128 devices in a mesh: seq: 32 (over y, x, core), heads: 4 (over z).
Axes of the slice: x: 4, y: 4, z: 4, core: 2. Of those that a mesh axis runs over, the one named last changes fastest.
Arguments:
- queries: bfloat16 [8192, 4096], P('seq', 'heads')
- keys: bfloat16 [8192, 4096], P('seq', 'heads')
- values: bfloat16 [8192, 4096], P('seq', 'heads'), may hold values from -6 to 6
- cca_queries: bfloat16 [8192, 4096], P('seq', 'heads')
- token_table: bfloat16 [128000, 2, 4096], P(('seq', 'heads'))
- neighbour_ids: int32 [128, 2, 128], P(('seq', 'heads')), may hold values from 0 to 127999, as said below
- doc_lengths: int32 [32], replicated, may hold values from 1 to 1792, 8192 in all
Outputs:
- attention_out: bfloat16 [8192, 4096], P('seq', 'heads')
- cca_out: bfloat16 [8192, 4096], P('seq', 'heads')
The draws below stay inside these ranges and needn't reach their ends.
Inputs may be any that keep to these rules, and one draw needn't show every extreme that they name: `neighbour_ids`: the 256 ids held by one device fall at most 4 times into the 1000 table rows of any one device; the rows of one device, the same for all, receive exactly 4 ids from every device. `doc_lengths`: the longest document has exactly 1792 tokens.
All inputs are finite; a program needn't handle non-finite values.
Results may differ from the reference program's by a relative error of at most 0.0044.
Values may be sent and summed in bfloat16 or wider, within the bound.
A program may use at most 192 MiB of HBM per device.

```python
import math
import jax
import jax.numpy as jnp
import numpy as np
from jax import lax

HEADS = 32
HS = 128
STRETCH = 64
NEIGH = 2
NLEN = 128
VOC_DEV = 1000
TOK_DEV = 256
TOKENS = 8192
STRETCHES = 128
HF = 4096
VOCAB = 128000
IDS_DEV = 256
CAP = 4
DOC_MAX = 1792
DOCS = 32
N_SEQ = 32


def key_field(key):
    return jax.random.normal(jax.random.fold_in(key, 11), (TOKENS, HF), jnp.float32)


def neighbour_field(key):
    base = jax.random.fold_in(key, 5)
    owners = VOCAB // VOC_DEV
    hot = jax.random.randint(jax.random.fold_in(base, 1), (), 0, owners)

    def one_block(block_key):
        first, second, third = jax.random.split(block_key, 3)
        rest = jnp.arange((owners - 1) * CAP, dtype=jnp.int32) // CAP
        rest = rest + (rest >= hot).astype(jnp.int32)
        rest = jax.random.permutation(first, rest)[:IDS_DEV - CAP]
        owner = jnp.concatenate([jnp.full((CAP,), hot, jnp.int32), rest])
        owner = jax.random.permutation(second, owner)
        row = jax.random.randint(third, (IDS_DEV,), 0, VOC_DEV)
        return owner * VOC_DEV + row
    block_keys = jax.random.split(jax.random.fold_in(base, 2), owners)
    return jax.vmap(one_block)(block_keys).reshape(STRETCHES, NEIGH, NLEN)


def table_rows(key, ids, spread):
    base = jax.random.fold_in(key, 7)

    def one_row(index):
        row_key = jax.random.fold_in(base, index)
        first, second, third = jax.random.split(row_key, 3)
        scale = 0.5 * jnp.exp(spread * jax.random.uniform(third, (), jnp.float32))
        key_part = scale * jax.random.normal(first, (HF,), jnp.float32)
        value_part = jax.random.normal(second, (HF,), jnp.float32)
        return (jnp.stack([key_part, value_part]), scale)
    return jax.vmap(one_row)(ids)


def draw_neighbour_ids(key, part):
    return neighbour_field(key)


def draw_token_table(key, part):
    spread = 0.0
    rows, scales = table_rows(key, jnp.arange(VOCAB, dtype=jnp.int32), spread)
    return rows.astype(jnp.bfloat16)


def draw_keys(key, part):
    return key_field(key).astype(jnp.bfloat16)


def draw_queries(key, part):
    key = jax.random.fold_in(key, 21)
    first = jax.random.fold_in(key, 0)
    return jax.random.normal(first, (TOKENS, HF), jnp.float32).astype(jnp.bfloat16)


def draw_cca_queries(key, part):
    key = jax.random.fold_in(key, 31)
    first = jax.random.fold_in(key, 0)
    return jax.random.normal(first, (TOKENS, HF), jnp.float32).astype(jnp.bfloat16)


def levels(rng, dims, pieces, smallest, high):
    level = 1.0
    for axis_at, parts in pieces:
        steps = jax.random.uniform(jax.random.fold_in(jax.random.fold_in(rng, 6), axis_at), (parts,), jnp.float32, smallest / len(pieces), high / len(pieces))
        level = level * jnp.repeat(jnp.exp(steps), dims[axis_at] // parts).reshape((-1,) + (1,) * (len(dims) - 1 - axis_at))
    return level


def profile(count, total, bound, skew):
    weights = [(1 << 20) // math.isqrt(grade ** skew) + 1 for grade in range(2, count + 1)]
    spare, counts = total - bound - (count - 1), [1] * (count - 1)
    while spare > 0:
        free = [i for i in range(count - 1) if counts[i] < bound]
        whole, left = sum([weights[i] for i in free]), spare
        for i in free:
            addition = min(bound - counts[i], max(1, left * weights[i] // whole), spare)
            counts[i] = counts[i] + addition
            spare = spare - addition
    return np.array([bound] + counts)


def uneven(key, count, total, bound, lean):
    if count == 2:
        one = jax.random.randint(key, (), max(1, total - bound), min(bound, total - 1) + 1)
        return jnp.stack([one, total - one])
    lengths = jnp.asarray(profile(count, total, bound, lean), jnp.int32)
    couples = (count - 1) // 2
    source_of, receiver = lengths[1:1 + 2 * couples:2], lengths[2:2 + 2 * couples:2]
    margin = jnp.minimum(source_of - 1, bound - receiver)
    moved = jax.random.randint(jax.random.fold_in(key, 1), (couples,), 0, 1 << 20) % (margin + 1)
    lengths = lengths.at[1:1 + 2 * couples:2].set(source_of - moved).at[2:2 + 2 * couples:2].set(receiver + moved)
    return lengths[jax.random.permutation(jax.random.fold_in(key, 2), count)]


def normal_values(rng, shape, width, reach, pieces=(), kind=jnp.bfloat16):
    entries = jax.random.normal(rng, shape, jnp.float32) * width
    if len(pieces) > 0:
        entries = levels(rng, shape, pieces, -0.22, 0.18) * entries
    return jnp.clip(entries, min=-reach, max=reach).astype(kind)


def setup_inputs(seed: int = 0) -> dict:
    arg_keys = jax.random.split(jax.random.key(seed), 8)
    queries = draw_queries(jax.random.fold_in(arg_keys[7], 71), 0)
    keys = draw_keys(jax.random.fold_in(arg_keys[7], 71), 0)
    values = normal_values(arg_keys[2], (TOKENS, HF), 1.0, 6.0, ((0, 32), (1, 4)))
    cca_queries = draw_cca_queries(jax.random.fold_in(arg_keys[7], 71), 0)
    token_table = draw_token_table(jax.random.fold_in(arg_keys[7], 71), 0)
    neighbour_ids = draw_neighbour_ids(jax.random.fold_in(arg_keys[7], 71), 0)
    doc_lengths = uneven(arg_keys[6], DOCS, TOKENS, DOC_MAX, 2).astype(jnp.int32)
    return dict(queries=queries, keys=keys, values=values, cca_queries=cca_queries, token_table=token_table, neighbour_ids=neighbour_ids, doc_lengths=doc_lengths)


NEG = -1e+30

def attend(query, key_block, value_block, allowed):
    scores = jnp.einsum('bqhd,bkhd->bhqk', query.astype(jnp.float32), key_block.astype(jnp.float32)) / math.sqrt(HS)
    scores = jnp.where(allowed[:, None], scores, NEG)
    top = lax.optimization_barrier(jnp.max(scores, axis=-1, keepdims=True))
    weights = jnp.where(allowed[:, None], jnp.exp(scores - top), 0.0)
    total = lax.optimization_barrier(jnp.sum(weights, axis=-1))
    rounded = lax.optimization_barrier(weights.astype(jnp.bfloat16))
    mixed = jnp.einsum('bhqk,bkhd->bqhd', rounded.astype(jnp.float32), value_block.astype(jnp.float32))
    return mixed / jnp.transpose(total, (0, 2, 1))[..., None]

def doc_of(positions, ends):
    return lax.optimization_barrier(jnp.sum((positions[:, None] >= ends[None, :]).astype(jnp.int32), axis=1))

def encode(rows):
    table_keys = rows[:, 0].reshape(NEIGH, NLEN, HEADS, HS)
    table_values = rows[:, 1].reshape(NEIGH, NLEN, HEADS, HS)
    mixed = attend(table_keys, table_keys, table_values, jnp.ones((1, NLEN, NLEN), bool))
    encoded_values = (table_values.astype(jnp.float32) + mixed).astype(jnp.bfloat16)
    return (table_keys.reshape(NEIGH * NLEN, HF), encoded_values.reshape(NEIGH * NLEN, HF))

def reference(queries, keys, values, cca_queries, token_table, neighbour_ids, doc_lengths):
    ends = jnp.cumsum(doc_lengths).astype(jnp.int32)
    key_pad = jnp.pad(keys, ((DOC_MAX, 0), (0, 0)))
    value_pad = jnp.pad(values, ((DOC_MAX, 0), (0, 0)))
    span = TOK_DEV + DOC_MAX

    def self_block(index):
        start = (index * TOK_DEV).astype(jnp.int32)
        query = lax.dynamic_slice_in_dim(queries, start, TOK_DEV, 0)
        key_block = lax.dynamic_slice_in_dim(key_pad, start, span, 0)
        value_block = lax.dynamic_slice_in_dim(value_pad, start, span, 0)
        query_pos = start + jnp.arange(TOK_DEV, dtype=jnp.int32)
        key_pos = start - DOC_MAX + jnp.arange(span, dtype=jnp.int32)
        allowed = (key_pos[None, :] <= query_pos[:, None]) & (key_pos[None, :] >= 0)
        allowed = allowed & (doc_of(query_pos, ends)[:, None] == doc_of(key_pos, ends)[None, :])
        result = attend(query.reshape(1, TOK_DEV, HEADS, HS), key_block.reshape(1, span, HEADS, HS), value_block.reshape(1, span, HEADS, HS), allowed[None])
        return result.reshape(TOK_DEV, HF).astype(jnp.bfloat16)
    attention_out = lax.map(self_block, jnp.arange(N_SEQ, dtype=jnp.int32)).reshape(TOKENS, HF)
    padded = jnp.pad(cca_queries, ((1, STRETCH - 1), (0, 0))).reshape(STRETCHES + 1, STRETCH, HEADS, HS)

    def cca_block(index):
        source = jnp.maximum(index - 1, 0)
        rows = token_table[neighbour_ids[source].reshape(-1)]
        enc_keys, enc_values = encode(rows)
        live = index > 0
        enc_keys = jnp.where(live, enc_keys, jnp.zeros_like(enc_keys))
        enc_values = jnp.where(live, enc_values, jnp.zeros_like(enc_values))
        result = attend(padded[index][None], enc_keys.reshape(1, NEIGH * NLEN, HEADS, HS), enc_values.reshape(1, NEIGH * NLEN, HEADS, HS), jnp.ones((1, STRETCH, NEIGH * NLEN), bool))
        return result.reshape(STRETCH, HF).astype(jnp.bfloat16)
    cca_full = lax.map(cca_block, jnp.arange(STRETCHES + 1, dtype=jnp.int32)).reshape((STRETCHES + 1) * STRETCH, HF)
    cca_out = cca_full[1:1 + TOKENS]
    return (attention_out, cca_out)
```

```python
import functools
import math

import jax
import jax.numpy as jnp
from jax import lax
from jax.experimental import pallas as pl
from jax.experimental.pallas import tpu as pltpu
from jax.sharding import PartitionSpec as P

MESH = pl.DeviceIdType.MESH
BF = jnp.bfloat16
F32 = jnp.float32
I32 = jnp.int32

HS = 128
STRETCH = 64
NLEN = 128
IDS = 256
CAP = 4
SEQ = 32
ZN = 4
DEV = SEQ * ZN
GROUP = 8
TOK = 256
HEADS_DEV = 8
SPAN = GROUP * TOK
HALO = 1792
WIN = HALO + TOK
WAVES = 8
PER_WAVE = SEQ // WAVES
NEG = -1e30
LOG2E = 1.4426950408889634
FACTOR = LOG2E / math.sqrt(HS)


def dot(a, b, contract=(1, 0)):
    return lax.dot_general(
        a, b, (((contract[0],), (contract[1],)), ((), ())), preferred_element_type=F32
    )


def iota(shape, dim):
    return lax.broadcasted_iota(I32, shape, dim)


def drain(ref, sem):
    pltpu.make_async_copy(ref, ref, sem).wait()


def kernel(
    q, k, v, cq, table, ids, lens, att, cca,
    tab, ids_all, plan_v, plan_s, send_buf, rows, zbuf, qh, kh, vh, oh, cqs, cqq, oc,
    tab_sem, id_send, id_recv, plan_sem, qkv_send, q_recv, k_recv, v_recv,
    halo_send, halo_recv, cq_send, cq_recv, row_send, row_recv,
    o_send, o_recv, oc_send, oc_recv,
):
    s = lax.axis_index("seq")
    z = lax.axis_index("heads")
    me = s * ZN + z
    y, x, c = s // 8, (s // 2) % 4, s % 2
    g = s % GROUP
    row = s // GROUP

    def place(y2, x2, c2):
        return (y2 * 4 + x2) * 2 + c2

    table_copy = pltpu.make_async_copy(table, tab, tab_sem)
    table_copy.start()

    barrier = pltpu.get_barrier_semaphore()

    def greet(i, carry):
        other = lax.rem(me + i, DEV)
        pl.semaphore_signal(
            barrier, inc=1, device_id=(other // ZN, lax.rem(other, ZN)), device_id_type=MESH
        )
        return carry

    lax.fori_loop(1, DEV, greet, 0)
    pl.semaphore_wait(barrier, DEV - 1)

    ids_all[me] = ids[0]
    first = []
    for n in range(1, 8):
        dc, dz = n // 4, n % 4
        s2, z2 = place(y, x, lax.rem(c + dc, 2)), lax.rem(z + dz, 4)
        copy = pltpu.make_async_remote_copy(
            ids_all.at[me], ids_all.at[me], id_send.at[n], id_recv.at[n],
            device_id=(s2, z2), device_id_type=MESH,
        )
        copy.start()
        first.append(copy)
    for copy in first:
        copy.wait()
    block = ids_all.at[pl.ds((y * 4 + x) * 8, 8)]
    second = []
    for n in range(1, 4):
        copy = pltpu.make_async_remote_copy(
            block, block, id_send.at[7 + n], id_recv.at[7 + n],
            device_id=(place(y, lax.rem(x + n, 4), c), z), device_id_type=MESH,
        )
        copy.start()
        second.append(copy)
    for copy in second:
        copy.wait()
    block = ids_all.at[pl.ds(y * 32, 32)]
    third = []
    for n in range(1, 4):
        copy = pltpu.make_async_remote_copy(
            block, block, id_send.at[10 + n], id_recv.at[10 + n],
            device_id=(place(lax.rem(y + n, 4), x, c), z), device_id_type=MESH,
        )
        copy.start()
        third.append(copy)

    for n in range(1, GROUP):
        to = lax.rem(g + n, GROUP)
        for src, dst, at, sem in (
            (q, qh, 0, q_recv), (k, kh, HALO, k_recv), (v, vh, HALO, v_recv),
        ):
            pltpu.make_async_remote_copy(
                src.at[:, pl.ds(to * HS, HS)], dst.at[pl.ds(at + g * TOK, TOK)],
                qkv_send, sem, device_id=(row * GROUP + to, z), device_id_type=MESH,
            ).start()
    for src, dst, at, sem in (
        (q, qh, 0, q_recv), (k, kh, HALO, k_recv), (v, vh, HALO, v_recv),
    ):
        pltpu.make_async_copy(
            src.at[:, pl.ds(g * HS, HS)], dst.at[pl.ds(at + g * TOK, TOK)], sem
        ).start()
    ahead = lax.rem(s + 1, SEQ)
    behind = lax.rem(s + SEQ - 1, SEQ)
    cq_copy = pltpu.make_async_remote_copy(
        cq.at[pl.ds(0, STRETCH)], cqs.at[pl.ds(TOK, STRETCH)], cq_send, cq_recv.at[0],
        device_id=(behind, z), device_id_type=MESH,
    )
    cq_copy.start()
    cq_own = pltpu.make_async_copy(cq, cqs.at[pl.ds(0, TOK)], cq_recv.at[1])
    cq_own.start()

    for copy in third:
        copy.wait()

    base = me * 1000
    row0 = ids_all[:, 0, :] - base
    row1 = ids_all[:, 1, :] - base
    mine0 = (row0 >= 0) & (row0 < 1000)
    mine1 = (row1 >= 0) & (row1 < 1000)
    flag0 = jnp.where(mine0, 1.0, 0.0).astype(BF)
    flag1 = jnp.where(mine1, 1.0, 0.0).astype(BF)
    tri = jnp.where(iota((HS, HS), 0) < iota((HS, HS), 1), 1.0, 0.0).astype(BF)
    full = jnp.ones((HS, HS), BF)
    rank0 = dot(flag0, tri)
    rank1 = dot(flag1, tri) + dot(flag0, full)
    plan = jnp.zeros((8, HS), I32)
    ones8 = jnp.ones((8, HS), BF)
    for n in range(CAP):
        pick = jnp.where(mine0 & (rank0 == float(n)), row0, 0) + jnp.where(
            mine1 & (rank1 == float(n)), row1, 0
        )
        high = dot(ones8, (pick >> 5).astype(F32).astype(BF), (1, 1))
        low = dot(ones8, (pick & 31).astype(F32).astype(BF), (1, 1))
        value = (high * 32.0 + low).astype(I32)
        plan = jnp.where(iota((8, HS), 0) == n, value, plan)
    plan_v[...] = plan
    plan_copy = pltpu.make_async_copy(plan_v, plan_s, plan_sem)
    plan_copy.start()
    plan_copy.wait()
    table_copy.wait()

    def column(t):
        dx = lax.rem(t, 4)
        dy = lax.rem(t // 4 + dx, 4)
        dc = t // 16
        return dx, dy, place(lax.rem(y + dy, 4), lax.rem(x + dx, 4), lax.rem(c + dc, 2))

    def fetch(to):
        for a in range(ZN):
            for n in range(CAP):
                found = tab[jnp.clip(plan_s[n, to * ZN + a], 0, 999)]
                send_buf[:, to, a, n * 16 : (n + 1) * 16, :] = found

    def post(to, z2, wave):
        pltpu.make_async_remote_copy(
            send_buf.at[z2, to], rows.at[:, me], row_send.at[wave], row_recv,
            device_id=(to, z2), device_id_type=MESH,
        ).start()

    def step(t, wave):
        dx, dy, to = column(t)
        fetch(to)
        for n in range(ZN):
            post(to, lax.rem(z + n + dx + dy, 4), wave)
        return wave

    fetch(s)
    pltpu.make_async_copy(send_buf.at[z, s], rows.at[:, me], row_recv).start()
    for n in range(1, ZN):
        post(s, lax.rem(z + n, 4), 0)
    lax.fori_loop(1, PER_WAVE, step, 0)

    def wave_out(wave):
        lax.fori_loop(wave * PER_WAVE, (wave + 1) * PER_WAVE, step, wave)

    wave_out(1)

    drain(qh, q_recv)
    drain(kh.at[pl.ds(HALO, SPAN)], k_recv)
    drain(vh.at[pl.ds(HALO, SPAN)], v_recv)
    next_row = lax.rem(row + 1, 4) * GROUP + g
    halos = []
    for n, ref in ((0, kh), (1, vh)):
        copy = pltpu.make_async_remote_copy(
            ref.at[pl.ds(HALO + TOK, HALO)], ref.at[pl.ds(0, HALO)],
            halo_send.at[n], halo_recv.at[n], device_id=(next_row, z), device_id_type=MESH,
        )
        copy.start()
        halos.append(copy)

    cq_copy.wait()
    cq_own.wait()
    up = jnp.where(iota((STRETCH, HS), 1) == iota((STRETCH, HS), 0) + 63, 1.0, 0.0).astype(BF)
    for a in range(4):
        moved = dot(up, cqs[a * STRETCH : a * STRETCH + 2 * STRETCH, :]).astype(BF)
        for h in range(HEADS_DEV):
            cqq[a, h] = moved[:, h * HS : (h + 1) * HS]

    for copy in halos:
        copy.wait()

    def self_block(i):
        first_query = row * SPAN + i * TOK
        query_pos = iota((1, TOK), 1) + first_query
        begin = jnp.zeros((1, TOK), I32)
        end = 0
        for d in range(32):
            end = end + lens[d]
            begin = jnp.where(query_pos >= end, end, begin)
        at = pl.multiple_of(i * TOK, TOK)
        key_pos = iota((WIN, TOK), 0) + (first_query - HALO)
        scores = dot(kh[pl.ds(at, WIN), :], qh[pl.ds(at, TOK), :], (1, 1))
        scores = jnp.where((key_pos >= begin) & (key_pos <= query_pos), scores, NEG)
        top = jnp.max(scores, axis=0, keepdims=True)
        weights = jnp.exp2((scores - top) * FACTOR)
        total = jnp.sum(weights, axis=0, keepdims=True)
        mixed = dot(vh[pl.ds(at, WIN), :], weights.astype(BF), (0, 0)) / total
        oh[pl.ds(at, TOK), :] = mixed.T.astype(BF)

    def self_out(i):
        at = pl.multiple_of(i * TOK, TOK)
        place_out = att.at[:, pl.ds(pl.multiple_of(g * HS, HS), HS)]

        @pl.when(i != g)
        def _():
            pltpu.make_async_remote_copy(
                oh.at[pl.ds(at, TOK)], place_out, o_send, o_recv,
                device_id=(row * GROUP + i, z), device_id_type=MESH,
            ).start()

        @pl.when(i == g)
        def _():
            pltpu.make_async_copy(oh.at[pl.ds(at, TOK)], place_out, o_recv).start()

    def wait_wave(wave):
        drain(send_buf.at[:, pl.ds(0, PER_WAVE)], row_send.at[wave])

    def turn(i, carry):
        self_block(i)
        self_out(i)

        @pl.when(i == 0)
        def _():
            drain(send_buf.at[0, pl.ds(0, 4 * PER_WAVE - 1)], row_send.at[0])

        @pl.when((i > 0) & (i < WAVES))
        def _():
            wait_wave(i)

        @pl.when(i + 2 < WAVES)
        def _():
            wave_out(i + 2)

        return carry

    lax.fori_loop(0, WAVES, turn, 0)

    drain(rows, row_recv)
    swap = jnp.where(
        (iota((256, 256), 0) // 16 == iota((256, 256), 1) % 16)
        & (iota((256, 256), 0) % 16 == iota((256, 256), 1) // 16),
        1.0, 0.0,
    ).astype(BF)

    def owner_of(value):
        return jnp.floor((value.astype(F32) + 0.5) * 0.001)

    def stretch(a):
        def turn_rows(n, carry):
            part = rows[a, pl.ds(n * 4, 4)].reshape(256, HS)
            turned = dot(swap, part).astype(BF)
            for h in range(HEADS_DEV):
                for kv in range(2):
                    piece = turned[(2 * h + kv) * 16 : (2 * h + kv + 1) * 16, :]
                    zbuf[h, pl.ds(n * 16, 16), kv * HS : (kv + 1) * HS] = piece
            return carry

        lax.fori_loop(0, 32, turn_rows, 0)
        wanted = ids_all[s * ZN + a]
        lane = [jnp.broadcast_to(owner_of(wanted[n : n + 1, :]), (HS, HS)) for n in range(2)]
        col = [jnp.transpose(w) for w in lane]
        before = iota((HS, HS), 1) < iota((HS, HS), 0)
        rank0 = jnp.sum(jnp.where((col[0] == lane[0]) & before, 1.0, 0.0), axis=1, keepdims=True)
        rank1 = jnp.sum(
            jnp.where((col[1] == lane[1]) & before, 1.0, 0.0)
            + jnp.where(col[1] == lane[0], 1.0, 0.0),
            axis=1, keepdims=True,
        )
        slot_no = iota((HS, DEV * CAP), 1).astype(F32)
        pick = jnp.concatenate(
            [
                jnp.where(slot_no == (owner[:, :1] * CAP + rank), 1.0, 0.0)
                for owner, rank in ((col[0], rank0), (col[1], rank1))
            ],
            axis=0,
        ).astype(BF)

        def heads(j, carry):
            for n in range(4):
                h = j * 4 + n
                both = dot(pick, zbuf[h]).astype(BF)
                keys, raw = both[:, :HS], both[:, HS:]
                encoded = []
                for m in range(2):
                    key, val = keys[m * NLEN : (m + 1) * NLEN], raw[m * NLEN : (m + 1) * NLEN]
                    scores = dot(key, key, (1, 1))
                    top = jnp.max(scores, axis=1, keepdims=True)
                    weights = jnp.exp2((scores - top) * FACTOR)
                    total = jnp.sum(weights, axis=1, keepdims=True)
                    mixed = dot(weights.astype(BF), val) / total
                    encoded.append((val.astype(F32) + mixed).astype(BF))
                vals = jnp.concatenate(encoded, axis=0)
                scores = dot(cqq[a, h], keys, (1, 1))
                top = jnp.max(scores, axis=1, keepdims=True)
                weights = jnp.exp2((scores - top) * FACTOR)
                total = jnp.sum(weights, axis=1, keepdims=True)
                oc[a + 1, h] = (dot(weights.astype(BF), vals) / total).astype(BF)
            return carry

        lax.fori_loop(0, 2, heads, 0)

    stretch(3)
    oc_copy = pltpu.make_async_remote_copy(
        oc.at[4], oc.at[0], oc_send, oc_recv, device_id=(ahead, z), device_id_type=MESH
    )
    oc_copy.start()

    def others(a, carry):
        stretch(a)
        return carry

    lax.fori_loop(0, 3, others, 0)
    oc_copy.wait()
    down = jnp.where(iota((STRETCH, HS), 1) == iota((STRETCH, HS), 0) + 1, 1.0, 0.0).astype(BF)
    for b in range(4):
        for h in range(HEADS_DEV):
            upper = oc[b, h]
            if b == 0:
                upper = jnp.where(s == 0, jnp.zeros_like(upper), upper)
            pair = jnp.concatenate([upper, oc[b + 1, h]], axis=0)
            cca[b * STRETCH : (b + 1) * STRETCH, h * HS : (h + 1) * HS] = dot(down, pair).astype(BF)

    drain(att, o_recv)
    for _ in range(GROUP - 1):
        drain(oh.at[pl.ds(0, TOK)], o_send)
    for _ in range(3):
        drain(qh.at[pl.ds(0, HALO)], qkv_send)


def body(queries, keys, values, cca_queries, token_table, neighbour_ids, doc_lengths):
    view = token_table.reshape(1000, 2, 32, HS).transpose(0, 2, 1, 3).reshape(1000, ZN, 16, HS)
    vmem = pl.BlockSpec(memory_space=pltpu.VMEM)
    hbm = pl.BlockSpec(memory_space=pl.ANY)
    smem = pl.BlockSpec(memory_space=pltpu.SMEM)
    dma = pltpu.SemaphoreType.DMA
    return pl.pallas_call(
        kernel,
        out_shape=[
            jax.ShapeDtypeStruct((TOK, HEADS_DEV * HS), BF),
            jax.ShapeDtypeStruct((TOK, HEADS_DEV * HS), BF),
        ],
        in_specs=[hbm, hbm, hbm, hbm, hbm, vmem, smem],
        out_specs=[hbm, vmem],
        scratch_shapes=[
            pltpu.VMEM((1000, ZN, 16, HS), BF),
            pltpu.VMEM((DEV, 2, HS), I32),
            pltpu.VMEM((8, HS), I32),
            pltpu.SMEM((8, HS), I32),
            pltpu.VMEM((ZN, SEQ, 4, 64, HS), BF),
            pltpu.VMEM((4, DEV, 64, HS), BF),
            pltpu.VMEM((HEADS_DEV, DEV * CAP, 2 * HS), BF),
            pltpu.VMEM((SPAN, HS), BF),
            pltpu.VMEM((HALO + SPAN, HS), BF),
            pltpu.VMEM((HALO + SPAN, HS), BF),
            pltpu.VMEM((SPAN, HS), BF),
            pltpu.VMEM((TOK + STRETCH, HEADS_DEV * HS), BF),
            pltpu.VMEM((4, HEADS_DEV, STRETCH, HS), BF),
            pltpu.VMEM((5, HEADS_DEV, STRETCH, HS), BF),
            dma, dma((14,)), dma((14,)), dma, dma, dma, dma, dma,
            dma((2,)), dma((2,)), dma, dma((2,)), dma((WAVES,)), dma,
            dma, dma, dma, dma,
        ],
        compiler_params=pltpu.CompilerParams(
            collective_id=0, has_side_effects=True, vmem_limit_bytes=60 * 1024 * 1024
        ),
        name="retrieval",
    )(queries, keys, values, cca_queries, view, neighbour_ids, doc_lengths)


def solution(mesh):
    in_specs = (
        P("seq", "heads"),
        P("seq", "heads"),
        P("seq", "heads"),
        P("seq", "heads"),
        P(("seq", "heads"), None, None),
        P(("seq", "heads"), None, None),
        P(),
    )
    out_specs = (P("seq", "heads"), P("seq", "heads"))

    def run(*args):
        return tuple(
            jax.shard_map(body, mesh=mesh, in_specs=in_specs, out_specs=out_specs, check_vma=False)(*args)
        )

    return run
```

```python
import functools
import math

import jax
import jax.numpy as jnp
from jax import lax
from jax.experimental import pallas as pl
from jax.experimental.pallas import tpu as pltpu
from jax.sharding import PartitionSpec as P

MESH = pl.DeviceIdType.MESH
BF = jnp.bfloat16
F32 = jnp.float32
I32 = jnp.int32

HS = 128
STRETCH = 64
NLEN = 128
IDS = 256
CAP = 4
SEQ = 32
ZN = 4
DEV = SEQ * ZN
GROUP = 8
TOK = 256
HEADS_DEV = 8
SPAN = GROUP * TOK
HALO = 1792
WIN = HALO + TOK
NEG = -1e30
LOG2E = 1.4426950408889634
FACTOR = LOG2E / math.sqrt(HS)


def dot(a, b, contract=(1, 0)):
    return lax.dot_general(
        a, b, (((contract[0],), (contract[1],)), ((), ())), preferred_element_type=F32
    )


def iota(shape, dim):
    return lax.broadcasted_iota(I32, shape, dim)


def drain(ref, sem):
    pltpu.make_async_copy(ref, ref, sem).wait()


ORDERS = (("y", "z", "x"), ("z", "x", "y"), ("x", "y", "z"), ("x", "y", "z"))


def kernel(
    q, k, v, cq, table, ids, lens, att, cca,
    tab, ids_all, plan_v, plan_s, out1, in1, in2, rows, picks, zbuf, qh, kh, vh, oh, cqs, cqq, oc,
    tab_sem, id_send, id_recv, plan_sem, qkv_send, q_recv, k_recv, v_recv,
    halo_send, halo_recv, cq_send, cq_recv, row_send, row_recv,
    o_send, o_recv, oc_send, oc_recv,
):
    s = lax.axis_index("seq")
    z = lax.axis_index("heads")
    me = s * ZN + z
    y, x, c = s // 8, lax.rem(s // 2, 4), lax.rem(s, 2)
    here = {"x": x, "y": y, "z": z}
    g = lax.rem(s, GROUP)
    row = y
    ahead = lax.rem(s + 1, SEQ)
    behind = lax.rem(s + SEQ - 1, SEQ)

    def device(x2=x, y2=y, z2=z, c2=c):
        return (y2 * 4 + x2) * 2 + c2, z2

    def along(axis, n, dc=0):
        to = lax.rem(here[axis] + n, 4)
        return to, device(**{axis + "2": to, "c2": lax.rem(c + dc, 2)})

    table_copy = pltpu.make_async_copy(table, tab, tab_sem)
    table_copy.start()

    barrier = pltpu.get_barrier_semaphore()
    partners = [along("x", 0, 1)[1]]
    for axis in ("x", "y", "z"):
        for n in range(1, 4):
            for dc in range(2):
                partners.append(along(axis, n, dc)[1])
    partners += [(ahead, z), (behind, z)]
    for other in partners:
        pl.semaphore_signal(barrier, inc=1, device_id=other, device_id_type=MESH)
    pl.semaphore_wait(barrier, len(partners))

    ids_all[me] = ids[0]

    def share(block, to, n):
        copy = pltpu.make_async_remote_copy(
            block, block, id_send.at[n], id_recv.at[n], device_id=to, device_id_type=MESH
        )
        copy.start()
        return copy

    first = [
        share(ids_all.at[me], along("z", n % 4, n // 4)[1], n) for n in range(1, 8)
    ]
    for copy in first:
        copy.wait()
    block = ids_all.at[pl.ds((y * 4 + x) * 8, 8)]
    second = [share(block, along("x", n)[1], 7 + n) for n in range(1, 4)]
    for copy in second:
        copy.wait()
    block = ids_all.at[pl.ds(y * 32, 32)]
    third = [share(block, along("y", n)[1], 10 + n) for n in range(1, 4)]

    for n in range(1, GROUP):
        to = lax.rem(g + n, GROUP)
        for src, dst, at, sem in (
            (q, qh, 0, q_recv), (k, kh, HALO, k_recv), (v, vh, HALO, v_recv),
        ):
            pltpu.make_async_remote_copy(
                src.at[:, pl.ds(to * HS, HS)], dst.at[pl.ds(at + g * TOK, TOK)],
                qkv_send, sem, device_id=(row * GROUP + to, z), device_id_type=MESH,
            ).start()
    for src, dst, at, sem in (
        (q, qh, 0, q_recv), (k, kh, HALO, k_recv), (v, vh, HALO, v_recv),
    ):
        pltpu.make_async_copy(
            src.at[:, pl.ds(g * HS, HS)], dst.at[pl.ds(at + g * TOK, TOK)], sem
        ).start()
    cq_copy = pltpu.make_async_remote_copy(
        cq.at[pl.ds(0, STRETCH)], cqs.at[pl.ds(TOK, STRETCH)], cq_send, cq_recv.at[0],
        device_id=(behind, z), device_id_type=MESH,
    )
    cq_copy.start()
    cq_own = pltpu.make_async_copy(cq, cqs.at[pl.ds(0, TOK)], cq_recv.at[1])
    cq_own.start()

    for copy in third:
        copy.wait()

    base = me * 1000
    row0 = ids_all[:, 0, :] - base
    row1 = ids_all[:, 1, :] - base
    mine0 = (row0 >= 0) & (row0 < 1000)
    mine1 = (row1 >= 0) & (row1 < 1000)
    flag0 = jnp.where(mine0, 1.0, 0.0).astype(BF)
    flag1 = jnp.where(mine1, 1.0, 0.0).astype(BF)
    tri = jnp.where(iota((HS, HS), 0) < iota((HS, HS), 1), 1.0, 0.0).astype(BF)
    full = jnp.ones((HS, HS), BF)
    rank0 = dot(flag0, tri)
    rank1 = dot(flag1, tri) + dot(flag0, full)
    plan = jnp.zeros((8, HS), I32)
    ones8 = jnp.ones((8, HS), BF)
    for n in range(CAP):
        pick = jnp.where(mine0 & (rank0 == float(n)), row0, 0) + jnp.where(
            mine1 & (rank1 == float(n)), row1, 0
        )
        high = dot(ones8, (pick >> 5).astype(F32).astype(BF), (1, 1))
        low = dot(ones8, (pick & 31).astype(F32).astype(BF), (1, 1))
        value = (high * 32.0 + low).astype(I32)
        plan = jnp.where(iota((8, HS), 0) == n, value, plan)
    plan_v[...] = plan
    plan_copy = pltpu.make_async_copy(plan_v, plan_s, plan_sem)
    plan_copy.start()
    plan_copy.wait()
    table_copy.wait()

    def fetch(a):
        order = ORDERS[a]

        def column(t, carry):
            spot = {"y": t // 8, "x": lax.rem(t // 2, 4), "z": slice(None)}
            c2 = lax.rem(t, 2)
            for n in range(CAP):
                found = tab[jnp.clip(plan_s[n, t * ZN + a], 0, 999)]
                at = (a, spot[order[0]], c2, spot[order[1]], spot[order[2]])
                out1[at + (slice(n * 16, (n + 1) * 16), slice(None))] = found
            return carry

        lax.fori_loop(0, SEQ, column, 0)

    def travel(a, phase):
        axis = ORDERS[a][phase]
        send, recv = row_send.at[a, phase], row_recv.at[a, phase]
        if phase == 0:
            hops = [(n, dc) for n in range(4) for dc in range(2)]
        else:
            hops = [(n, 0) for n in range(4)]
        for n, dc in hops[1:] + hops[:1]:
            to, dev = along(axis, n, dc)
            if phase == 0:
                src, dst = out1.at[a, to, lax.rem(c + dc, 2)], in1.at[a, here[axis] * 2 + c]
            elif phase == 1:
                src, dst = in1.at[a, :, to], in2.at[a, here[axis]]
            else:
                src, dst = in2.at[a, :, :, to], rows.at[a, here[axis]]
            if (n, dc) == (0, 0):
                pltpu.make_async_copy(src, dst, recv).start()
            else:
                pltpu.make_async_remote_copy(
                    src, dst, send, recv, device_id=dev, device_id_type=MESH
                ).start()

    landed = (in1, in2, rows)

    def arrive(a, phase):
        drain(landed[phase].at[a], row_recv.at[a, phase])

    for a in (3, 0, 1):
        fetch(a)
        travel(a, 0)
    fetch(2)

    def owner_of(value):
        return jnp.floor((value.astype(F32) + 0.5) * 0.001).astype(I32)

    before = iota((HS, HS), 1) < iota((HS, HS), 0)
    slot_no = iota((HS, DEV * CAP), 1).astype(F32)
    for a in range(4):
        wanted = owner_of(ids_all[s * ZN + a])
        lane = [jnp.broadcast_to(wanted[n : n + 1, :], (HS, HS)) for n in range(2)]
        col = [jnp.transpose(w) for w in lane]
        rank0 = jnp.sum(jnp.where((col[0] == lane[0]) & before, 1.0, 0.0), axis=1, keepdims=True)
        rank1 = jnp.sum(
            jnp.where((col[1] == lane[1]) & before, 1.0, 0.0)
            + jnp.where(col[1] == lane[0], 1.0, 0.0),
            axis=1, keepdims=True,
        )
        for n, rank in ((0, rank0), (1, rank1)):
            owner = col[n][:, :1]
            part = {"z": owner & 3, "x": (owner >> 3) & 3, "y": owner >> 5}
            order = ORDERS[a]
            where = part[order[2]] * 32 + part[order[1]] * 8 + part[order[0]] * 2 + ((owner >> 2) & 1)
            slot = where.astype(F32) * CAP + rank
            picks[a, n * HS : (n + 1) * HS, :] = jnp.where(slot_no == slot, 1.0, 0.0).astype(BF)

    drain(qh, q_recv)
    drain(kh.at[pl.ds(HALO, SPAN)], k_recv)
    drain(vh.at[pl.ds(HALO, SPAN)], v_recv)
    halos = []
    for n, ref in ((0, kh), (1, vh)):
        copy = pltpu.make_async_remote_copy(
            ref.at[pl.ds(HALO + TOK, HALO)], ref.at[pl.ds(0, HALO)],
            halo_send.at[n], halo_recv.at[n], device_id=along("y", 1)[1], device_id_type=MESH,
        )
        copy.start()
        halos.append(copy)

    cq_copy.wait()
    cq_own.wait()
    up = jnp.where(iota((STRETCH, HS), 1) == iota((STRETCH, HS), 0) + 63, 1.0, 0.0).astype(BF)
    for a in range(4):
        moved = dot(up, cqs[a * STRETCH : a * STRETCH + 2 * STRETCH, :]).astype(BF)
        for h in range(HEADS_DEV):
            cqq[a, h] = moved[:, h * HS : (h + 1) * HS]

    for a, b in ((3, 2), (0, None), (1, None)):
        arrive(a, 0)
        travel(a, 1)
        if b is not None:
            travel(b, 0)

    for copy in halos:
        copy.wait()

    def self_block(i):
        first_query = row * SPAN + i * TOK
        query_pos = iota((1, TOK), 1) + first_query
        begin = jnp.zeros((1, TOK), I32)
        end = 0
        for d in range(32):
            end = end + lens[d]
            begin = jnp.where(query_pos >= end, end, begin)
        at = pl.multiple_of(i * TOK, TOK)
        key_pos = iota((WIN, TOK), 0) + (first_query - HALO)
        scores = dot(kh[pl.ds(at, WIN), :], qh[pl.ds(at, TOK), :], (1, 1))
        scores = jnp.where((key_pos >= begin) & (key_pos <= query_pos), scores, NEG)
        top = jnp.max(scores, axis=0, keepdims=True)
        weights = jnp.exp2((scores - top) * FACTOR)
        total = jnp.sum(weights, axis=0, keepdims=True)
        mixed = dot(vh[pl.ds(at, WIN), :], weights.astype(BF), (0, 0)) / total
        oh[pl.ds(at, TOK), :] = mixed.T.astype(BF)

    def self_out(i):
        at = pl.multiple_of(i * TOK, TOK)
        place_out = att.at[:, pl.ds(pl.multiple_of(g * HS, HS), HS)]

        @pl.when(i != g)
        def _():
            pltpu.make_async_remote_copy(
                oh.at[pl.ds(at, TOK)], place_out, o_send, o_recv,
                device_id=(row * GROUP + i, z), device_id_type=MESH,
            ).start()

        @pl.when(i == g)
        def _():
            pltpu.make_async_copy(oh.at[pl.ds(at, TOK)], place_out, o_recv).start()

    def turn(i, carry):
        self_block(i)
        self_out(i)
        return carry

    lax.fori_loop(0, 3, turn, 0)
    arrive(3, 1)
    travel(3, 2)
    arrive(2, 0)
    travel(2, 1)
    arrive(0, 1)
    travel(0, 2)
    arrive(1, 1)
    travel(1, 2)
    lax.fori_loop(3, GROUP, turn, 0)
    arrive(2, 1)
    travel(2, 2)

    swap = jnp.where(
        (iota((256, 256), 0) // 16 == iota((256, 256), 1) % 16)
        & (iota((256, 256), 0) % 16 == iota((256, 256), 1) // 16),
        1.0, 0.0,
    ).astype(BF)

    def stretch(a):
        def turn_rows(n, carry):
            for m in range(2):
                spot = n * 4 + 2 * m
                parts = [
                    rows[a, n // 2, lax.rem(n, 2) * 2 + m, j * 4 : (j + 1) * 4].reshape(256, HS)
                    for j in range(2)
                ]
                turned = dot(swap, jnp.concatenate(parts, axis=1)).astype(BF)
                for j in range(2):
                    for h in range(HEADS_DEV):
                        for kv in range(2):
                            piece = turned[
                                (2 * h + kv) * 16 : (2 * h + kv + 1) * 16, j * HS : (j + 1) * HS
                            ]
                            zbuf[h, pl.ds((spot + j) * 16, 16), kv * HS : (kv + 1) * HS] = piece
            return carry

        lax.fori_loop(0, 8, turn_rows, 0)
        pick = picks[a]

        def heads(j, carry):
            for n in range(4):
                h = j * 4 + n
                both = dot(pick, zbuf[h]).astype(BF)
                keys, raw = both[:, :HS], both[:, HS:]
                encoded = []
                for m in range(2):
                    key, val = keys[m * NLEN : (m + 1) * NLEN], raw[m * NLEN : (m + 1) * NLEN]
                    scores = dot(key, key, (1, 1))
                    top = jnp.max(scores, axis=1, keepdims=True)
                    weights = jnp.exp2((scores - top) * FACTOR)
                    total = jnp.sum(weights, axis=1, keepdims=True)
                    mixed = dot(weights.astype(BF), val) / total
                    encoded.append((val.astype(F32) + mixed).astype(BF))
                vals = jnp.concatenate(encoded, axis=0)
                scores = dot(cqq[a, h], keys, (1, 1))
                top = jnp.max(scores, axis=1, keepdims=True)
                weights = jnp.exp2((scores - top) * FACTOR)
                total = jnp.sum(weights, axis=1, keepdims=True)
                oc[a + 1, h] = (dot(weights.astype(BF), vals) / total).astype(BF)
            return carry

        lax.fori_loop(0, 2, heads, 0)

    arrive(3, 2)
    stretch(3)
    oc_copy = pltpu.make_async_remote_copy(
        oc.at[4], oc.at[0], oc_send, oc_recv, device_id=(ahead, z), device_id_type=MESH
    )
    oc_copy.start()
    for a in (0, 1, 2):
        arrive(a, 2)
        stretch(a)
    oc_copy.wait()
    down = jnp.where(iota((STRETCH, HS), 1) == iota((STRETCH, HS), 0) + 1, 1.0, 0.0).astype(BF)
    for b in range(4):
        for h in range(HEADS_DEV):
            upper = oc[b, h]
            if b == 0:
                upper = jnp.where(s == 0, jnp.zeros_like(upper), upper)
            pair = jnp.concatenate([upper, oc[b + 1, h]], axis=0)
            cca[b * STRETCH : (b + 1) * STRETCH, h * HS : (h + 1) * HS] = dot(down, pair).astype(BF)

    drain(att, o_recv)
    for _ in range(GROUP - 1):
        drain(oh.at[pl.ds(0, TOK)], o_send)
    for _ in range(3):
        drain(qh.at[pl.ds(0, HALO)], qkv_send)
    for a in range(4):
        drain(in1.at[a, pl.ds(0, 7)], row_send.at[a, 0])
        drain(in2.at[a, pl.ds(0, 3)], row_send.at[a, 1])
        drain(rows.at[a, pl.ds(0, 3)], row_send.at[a, 2])


def body(queries, keys, values, cca_queries, token_table, neighbour_ids, doc_lengths):
    view = token_table.reshape(1000, 2, 32, HS).transpose(0, 2, 1, 3).reshape(1000, ZN, 16, HS)
    vmem = pl.BlockSpec(memory_space=pltpu.VMEM)
    hbm = pl.BlockSpec(memory_space=pl.ANY)
    smem = pl.BlockSpec(memory_space=pltpu.SMEM)
    dma = pltpu.SemaphoreType.DMA
    return pl.pallas_call(
        kernel,
        out_shape=[
            jax.ShapeDtypeStruct((TOK, HEADS_DEV * HS), BF),
            jax.ShapeDtypeStruct((TOK, HEADS_DEV * HS), BF),
        ],
        in_specs=[hbm, hbm, hbm, hbm, hbm, vmem, smem],
        out_specs=[hbm, vmem],
        scratch_shapes=[
            pltpu.VMEM((1000, ZN, 16, HS), BF),
            pltpu.VMEM((DEV, 2, HS), I32),
            pltpu.VMEM((8, HS), I32),
            pltpu.SMEM((8, HS), I32),
            pltpu.VMEM((4, 4, 2, 4, 4, 64, HS), BF),
            pltpu.VMEM((4, 8, 4, 4, 64, HS), BF),
            pltpu.VMEM((4, 4, 8, 4, 64, HS), BF),
            pltpu.VMEM((4, 4, 4, 8, 64, HS), BF),
            pltpu.VMEM((4, IDS, DEV * CAP), BF),
            pltpu.VMEM((HEADS_DEV, DEV * CAP, 2 * HS), BF),
            pltpu.VMEM((SPAN, HS), BF),
            pltpu.VMEM((HALO + SPAN, HS), BF),
            pltpu.VMEM((HALO + SPAN, HS), BF),
            pltpu.VMEM((SPAN, HS), BF),
            pltpu.VMEM((TOK + STRETCH, HEADS_DEV * HS), BF),
            pltpu.VMEM((4, HEADS_DEV, STRETCH, HS), BF),
            pltpu.VMEM((5, HEADS_DEV, STRETCH, HS), BF),
            dma, dma((14,)), dma((14,)), dma, dma, dma, dma, dma,
            dma((2,)), dma((2,)), dma, dma((2,)), dma((4, 3)), dma((4, 3)),
            dma, dma, dma, dma,
        ],
        compiler_params=pltpu.CompilerParams(
            collective_id=0, has_side_effects=True, vmem_limit_bytes=60 * 1024 * 1024
        ),
        name="retrieval",
    )(queries, keys, values, cca_queries, view, neighbour_ids, doc_lengths)


def solution(mesh):
    in_specs = (
        P("seq", "heads"),
        P("seq", "heads"),
        P("seq", "heads"),
        P("seq", "heads"),
        P(("seq", "heads"), None, None),
        P(("seq", "heads"), None, None),
        P(),
    )
    out_specs = (P("seq", "heads"), P("seq", "heads"))

    def run(*args):
        return tuple(
            jax.shard_map(body, mesh=mesh, in_specs=in_specs, out_specs=out_specs, check_vma=False)(*args)
        )

    return run
```

```python
import functools
import math

import jax
import jax.numpy as jnp
from jax import lax
from jax.experimental import pallas as pl
from jax.experimental.pallas import tpu as pltpu
from jax.sharding import PartitionSpec as P

MESH = pl.DeviceIdType.MESH
BF = jnp.bfloat16
F32 = jnp.float32
I32 = jnp.int32

HS = 128
STRETCH = 64
NLEN = 128
IDS = 256
CAP = 4
SEQ = 32
ZN = 4
DEV = SEQ * ZN
GROUP = 8
TOK = 256
HEADS_DEV = 8
SPAN = GROUP * TOK
HALO = 1792
WIN = HALO + TOK
NEG = -1e30
LOG2E = 1.4426950408889634
FACTOR = LOG2E / math.sqrt(HS)


def dot(a, b, contract=(1, 0)):
    return lax.dot_general(
        a, b, (((contract[0],), (contract[1],)), ((), ())), preferred_element_type=F32
    )


def iota(shape, dim):
    return lax.broadcasted_iota(I32, shape, dim)


def drain(ref, sem):
    pltpu.make_async_copy(ref, ref, sem).wait()


ROUTES = (("x", "y", "z"), ("y", "z", "x"), ("z", "x", "y"))
GROUPS = ((0, 2), (2, 1), (3, 1))


def route(a, n):
    return ROUTES[(a + n) % 3]


def kernel(
    q, k, v, cq, table, ids, lens, att, cca,
    tab, ids_all, plan_v, plan_s, out1, in1, in2, rows, picks, zbuf, qh, kh, vh, oh, cqs, cqq, oc,
    tab_sem, id_send, id_recv, plan_sem, qkv_send, q_recv, k_recv, v_recv,
    halo_send, halo_recv, cq_send, cq_recv, row_send, row_recv,
    o_send, o_recv, oc_send, oc_recv,
):
    s = lax.axis_index("seq")
    z = lax.axis_index("heads")
    me = s * ZN + z
    y, x, c = s // 8, lax.rem(s // 2, 4), lax.rem(s, 2)
    here = {"x": x, "y": y, "z": z}
    g = lax.rem(s, GROUP)
    row = y
    ahead = lax.rem(s + 1, SEQ)
    behind = lax.rem(s + SEQ - 1, SEQ)

    def device(x2=x, y2=y, z2=z, c2=c):
        return (y2 * 4 + x2) * 2 + c2, z2

    def along(axis, n, dc=0):
        to = lax.rem(here[axis] + n, 4)
        return to, device(**{axis + "2": to, "c2": lax.rem(c + dc, 2)})

    def across(dy, dx):
        return device(x2=lax.rem(x + dx, 4), y2=lax.rem(y + dy, 4))

    table_copy = pltpu.make_async_copy(table, tab, tab_sem)
    table_copy.start()

    barrier = pltpu.get_barrier_semaphore()
    partners = [along("x", 0, 1)[1]]
    for axis in ("x", "y", "z"):
        for n in range(1, 4):
            for dc in range(2):
                partners.append(along(axis, n, dc)[1])
    partners += [across(dy, dx) for dy in range(1, 4) for dx in range(1, 4)]
    partners += [(ahead, z), (behind, z)]
    for other in partners:
        pl.semaphore_signal(barrier, inc=1, device_id=other, device_id_type=MESH)
    pl.semaphore_wait(barrier, len(partners))

    ids_all[me] = ids[0]

    def share(block, to, n):
        copy = pltpu.make_async_remote_copy(
            block, block, id_send.at[n], id_recv.at[n], device_id=to, device_id_type=MESH
        )
        copy.start()
        return copy

    first = [
        share(ids_all.at[me], along("z", n % 4, n // 4)[1], n) for n in range(1, 8)
    ]
    for copy in first:
        copy.wait()
    block = ids_all.at[pl.ds((y * 4 + x) * 8, 8)]
    second = [share(block, across(n // 4, n % 4), 7 + n) for n in range(1, 16)]

    for n in range(1, GROUP):
        to = lax.rem(g + n, GROUP)
        for src, dst, at, sem in (
            (q, qh, 0, q_recv), (k, kh, HALO, k_recv), (v, vh, HALO, v_recv),
        ):
            pltpu.make_async_remote_copy(
                src.at[:, pl.ds(to * HS, HS)], dst.at[pl.ds(at + g * TOK, TOK)],
                qkv_send, sem, device_id=(row * GROUP + to, z), device_id_type=MESH,
            ).start()
    for src, dst, at, sem in (
        (q, qh, 0, q_recv), (k, kh, HALO, k_recv), (v, vh, HALO, v_recv),
    ):
        pltpu.make_async_copy(
            src.at[:, pl.ds(g * HS, HS)], dst.at[pl.ds(at + g * TOK, TOK)], sem
        ).start()
    cq_copy = pltpu.make_async_remote_copy(
        cq.at[pl.ds(0, STRETCH)], cqs.at[pl.ds(TOK, STRETCH)], cq_send, cq_recv.at[0],
        device_id=(behind, z), device_id_type=MESH,
    )
    cq_copy.start()
    cq_own = pltpu.make_async_copy(cq, cqs.at[pl.ds(0, TOK)], cq_recv.at[1])
    cq_own.start()

    for copy in second:
        copy.wait()

    base = me * 1000
    row0 = ids_all[:, 0, :] - base
    row1 = ids_all[:, 1, :] - base
    mine0 = (row0 >= 0) & (row0 < 1000)
    mine1 = (row1 >= 0) & (row1 < 1000)
    flag0 = jnp.where(mine0, 1.0, 0.0).astype(BF)
    flag1 = jnp.where(mine1, 1.0, 0.0).astype(BF)
    tri = jnp.where(iota((HS, HS), 0) < iota((HS, HS), 1), 1.0, 0.0).astype(BF)
    full = jnp.ones((HS, HS), BF)
    rank0 = dot(flag0, tri)
    rank1 = dot(flag1, tri) + dot(flag0, full)
    plan = jnp.zeros((8, HS), I32)
    ones8 = jnp.ones((8, HS), BF)
    for n in range(CAP):
        pick = jnp.where(mine0 & (rank0 == float(n)), row0, 0) + jnp.where(
            mine1 & (rank1 == float(n)), row1, 0
        )
        high = dot(ones8, (pick >> 5).astype(F32).astype(BF), (1, 1))
        low = dot(ones8, (pick & 31).astype(F32).astype(BF), (1, 1))
        value = (high * 32.0 + low).astype(I32)
        plan = jnp.where(iota((8, HS), 0) == n, value, plan)
    plan_v[...] = plan
    plan_copy = pltpu.make_async_copy(plan_v, plan_s, plan_sem)
    plan_copy.start()
    plan_copy.wait()
    table_copy.wait()

    def fetch(a):
        def column(t, carry):
            spot = {"y": t // 8, "x": lax.rem(t // 2, 4), "z": slice(None)}
            c2 = lax.rem(t, 2)
            for i, (low, count) in enumerate(GROUPS):
                order = route(a, i)
                at = (a, spot[order[0]], c2, spot[order[1]], spot[order[2]])
                for n in range(low, low + count):
                    found = tab[jnp.clip(plan_s[n, t * ZN + a], 0, 999)]
                    out1[at + (slice(n * 16, (n + 1) * 16), slice(None))] = found
            return carry

        lax.fori_loop(0, SEQ, column, 0)

    def part_of(i):
        low, count = GROUPS[i]
        return pl.ds(low * 16, count * 16)

    def travel(a, phase):
        everything = slice(None)
        for i in range(3):
            axis, part = route(a, i)[phase], part_of(i)
            send, recv = row_send.at[a, phase, i], row_recv.at[a, phase, i]
            if phase == 0:
                hops = [(n, dc) for n in range(4) for dc in range(2)]
            else:
                hops = [(n, 0) for n in range(4)]
            for n, dc in hops[1:] + hops[:1]:
                to, dev = along(axis, n, dc)
                if phase == 0:
                    src = out1.at[a, to, lax.rem(c + dc, 2), :, :, part]
                    dst = in1.at[a, here[axis] * 2 + c, :, :, part]
                elif phase == 1:
                    src = in1.at[a, :, to, :, part]
                    dst = in2.at[a, here[axis], :, :, part]
                else:
                    src = in2.at[a, :, :, to, part]
                    dst = rows.at[a, here[axis], :, :, part]
                if (n, dc) == (0, 0):
                    pltpu.make_async_copy(src, dst, recv).start()
                else:
                    pltpu.make_async_remote_copy(
                        src, dst, send, recv, device_id=dev, device_id_type=MESH
                    ).start()

    landed = (in1, in2, rows)

    def arrive(a, phase):
        for i in range(3):
            drain(landed[phase].at[a, :, :, :, part_of(i)], row_recv.at[a, phase, i])

    for a in (3, 0, 1):
        fetch(a)
        travel(a, 0)
    fetch(2)

    def owner_of(value):
        return jnp.floor((value.astype(F32) + 0.5) * 0.001).astype(I32)

    before = iota((HS, HS), 1) < iota((HS, HS), 0)
    slot_no = iota((HS, DEV * CAP), 1).astype(F32)
    for a in range(4):
        wanted = owner_of(ids_all[s * ZN + a])
        lane = [jnp.broadcast_to(wanted[n : n + 1, :], (HS, HS)) for n in range(2)]
        col = [jnp.transpose(w) for w in lane]
        rank0 = jnp.sum(jnp.where((col[0] == lane[0]) & before, 1.0, 0.0), axis=1, keepdims=True)
        rank1 = jnp.sum(
            jnp.where((col[1] == lane[1]) & before, 1.0, 0.0)
            + jnp.where(col[1] == lane[0], 1.0, 0.0),
            axis=1, keepdims=True,
        )
        for n, rank in ((0, rank0), (1, rank1)):
            owner = col[n][:, :1]
            part = {"z": owner & 3, "x": (owner >> 3) & 3, "y": owner >> 5}
            spots = []
            for i in range(3):
                order = route(a, i)
                spot = part[order[2]] * 32 + part[order[1]] * 8 + part[order[0]] * 2
                spots.append((spot + ((owner >> 2) & 1)).astype(F32))
            spot = jnp.where(rank < 2.0, spots[0], jnp.where(rank < 3.0, spots[1], spots[2]))
            slot = spot * CAP + rank
            picks[a, n * HS : (n + 1) * HS, :] = jnp.where(slot_no == slot, 1.0, 0.0).astype(BF)

    drain(qh, q_recv)
    drain(kh.at[pl.ds(HALO, SPAN)], k_recv)
    drain(vh.at[pl.ds(HALO, SPAN)], v_recv)
    halos = []
    for n, ref in ((0, kh), (1, vh)):
        copy = pltpu.make_async_remote_copy(
            ref.at[pl.ds(HALO + TOK, HALO)], ref.at[pl.ds(0, HALO)],
            halo_send.at[n], halo_recv.at[n], device_id=along("y", 1)[1], device_id_type=MESH,
        )
        copy.start()
        halos.append(copy)

    cq_copy.wait()
    cq_own.wait()
    up = jnp.where(iota((STRETCH, HS), 1) == iota((STRETCH, HS), 0) + 63, 1.0, 0.0).astype(BF)
    for a in range(4):
        moved = dot(up, cqs[a * STRETCH : a * STRETCH + 2 * STRETCH, :]).astype(BF)
        for h in range(HEADS_DEV):
            cqq[a, h] = moved[:, h * HS : (h + 1) * HS]

    def onward(a, phase):
        arrive(a, phase)
        travel(a, phase + 1)

    onward(3, 0)
    travel(2, 0)
    onward(0, 0)

    for copy in halos:
        copy.wait()

    def self_block(i):
        first_query = row * SPAN + i * TOK
        query_pos = iota((1, TOK), 1) + first_query
        begin = jnp.zeros((1, TOK), I32)
        end = 0
        for d in range(32):
            end = end + lens[d]
            begin = jnp.where(query_pos >= end, end, begin)
        at = pl.multiple_of(i * TOK, TOK)
        key_pos = iota((WIN, TOK), 0) + (first_query - HALO)
        scores = dot(kh[pl.ds(at, WIN), :], qh[pl.ds(at, TOK), :], (1, 1))
        scores = jnp.where((key_pos >= begin) & (key_pos <= query_pos), scores, NEG)
        top = jnp.max(scores, axis=0, keepdims=True)
        weights = jnp.exp2((scores - top) * FACTOR)
        total = jnp.sum(weights, axis=0, keepdims=True)
        mixed = dot(vh[pl.ds(at, WIN), :], weights.astype(BF), (0, 0)) / total
        oh[pl.ds(at, TOK), :] = mixed.T.astype(BF)

    def self_out(i):
        at = pl.multiple_of(i * TOK, TOK)
        place_out = att.at[:, pl.ds(pl.multiple_of(g * HS, HS), HS)]

        @pl.when(i != g)
        def _():
            pltpu.make_async_remote_copy(
                oh.at[pl.ds(at, TOK)], place_out, o_send, o_recv,
                device_id=(row * GROUP + i, z), device_id_type=MESH,
            ).start()

        @pl.when(i == g)
        def _():
            pltpu.make_async_copy(oh.at[pl.ds(at, TOK)], place_out, o_recv).start()

    def turn(i, carry):
        self_block(i)
        self_out(i)
        return carry

    lax.fori_loop(0, 2, turn, 0)
    onward(3, 1)
    lax.fori_loop(2, 4, turn, 0)
    onward(1, 0)
    lax.fori_loop(4, 6, turn, 0)
    onward(0, 1)
    lax.fori_loop(6, 8, turn, 0)

    swap = jnp.where(
        (iota((256, 256), 0) // 16 == iota((256, 256), 1) % 16)
        & (iota((256, 256), 0) % 16 == iota((256, 256), 1) // 16),
        1.0, 0.0,
    ).astype(BF)

    def stretch(a):
        def turn_rows(n, carry):
            for m in range(8):
                spot = n * 16 + 2 * m
                parts = [
                    rows[a, n * 2 + m // 4, m % 4, j * 4 : (j + 1) * 4].reshape(256, HS)
                    for j in range(2)
                ]
                turned = dot(swap, jnp.concatenate(parts, axis=1)).astype(BF)
                for j in range(2):
                    for h in range(HEADS_DEV):
                        for kv in range(2):
                            piece = turned[
                                (2 * h + kv) * 16 : (2 * h + kv + 1) * 16, j * HS : (j + 1) * HS
                            ]
                            zbuf[h, pl.ds((spot + j) * 16, 16), kv * HS : (kv + 1) * HS] = piece
            return carry

        lax.fori_loop(0, 2, turn_rows, 0)
        pick = picks[a]

        def weigh(scores):
            weights = jnp.exp2((scores - jnp.max(scores, axis=1, keepdims=True)) * FACTOR)
            return weights, jnp.sum(weights, axis=1, keepdims=True)

        both = [dot(pick, zbuf[h]).astype(BF) for h in range(HEADS_DEV)]
        keys = [pair[:, :HS] for pair in both]
        halves = [
            [(pair[m * NLEN : (m + 1) * NLEN, :HS], pair[m * NLEN : (m + 1) * NLEN, HS:]) for m in range(2)]
            for pair in both
        ]
        enc_scores = [[dot(key, key, (1, 1)) for key, _ in two] for two in halves]
        cca_scores = [dot(cqq[a, h], keys[h], (1, 1)) for h in range(HEADS_DEV)]
        enc = [[weigh(scores) for scores in two] for two in enc_scores]
        cross = [weigh(scores) for scores in cca_scores]
        for h in range(HEADS_DEV):
            encoded = []
            for (weights, total), (_, val) in zip(enc[h], halves[h]):
                mixed = dot(weights.astype(BF), val) / total
                encoded.append((val.astype(F32) + mixed).astype(BF))
            weights, total = cross[h]
            mixed = dot(weights.astype(BF), jnp.concatenate(encoded, axis=0)) / total
            oc[a + 1, h] = mixed.astype(BF)

    arrive(3, 2)
    onward(2, 0)
    stretch(3)
    oc_copy = pltpu.make_async_remote_copy(
        oc.at[4], oc.at[0], oc_send, oc_recv, device_id=(ahead, z), device_id_type=MESH
    )
    oc_copy.start()
    onward(1, 1)
    arrive(0, 2)
    stretch(0)
    onward(2, 1)
    arrive(1, 2)
    stretch(1)
    arrive(2, 2)
    stretch(2)
    oc_copy.wait()
    down = jnp.where(iota((STRETCH, HS), 1) == iota((STRETCH, HS), 0) + 1, 1.0, 0.0).astype(BF)
    for b in range(4):
        for h in range(HEADS_DEV):
            upper = oc[b, h]
            if b == 0:
                upper = jnp.where(s == 0, jnp.zeros_like(upper), upper)
            pair = jnp.concatenate([upper, oc[b + 1, h]], axis=0)
            cca[b * STRETCH : (b + 1) * STRETCH, h * HS : (h + 1) * HS] = dot(down, pair).astype(BF)

    drain(att, o_recv)
    for _ in range(GROUP - 1):
        drain(oh.at[pl.ds(0, TOK)], o_send)
    for _ in range(3):
        drain(qh.at[pl.ds(0, HALO)], qkv_send)
    for a in range(4):
        for i in range(3):
            part = part_of(i)
            drain(in1.at[a, pl.ds(0, 7), :, :, part], row_send.at[a, 0, i])
            drain(in2.at[a, pl.ds(0, 3), :, :, part], row_send.at[a, 1, i])
            drain(rows.at[a, pl.ds(0, 3), :, :, part], row_send.at[a, 2, i])


def body(queries, keys, values, cca_queries, token_table, neighbour_ids, doc_lengths):
    view = token_table.reshape(1000, 2, 32, HS).transpose(0, 2, 1, 3).reshape(1000, ZN, 16, HS)
    vmem = pl.BlockSpec(memory_space=pltpu.VMEM)
    hbm = pl.BlockSpec(memory_space=pl.ANY)
    smem = pl.BlockSpec(memory_space=pltpu.SMEM)
    dma = pltpu.SemaphoreType.DMA
    return pl.pallas_call(
        kernel,
        out_shape=[
            jax.ShapeDtypeStruct((TOK, HEADS_DEV * HS), BF),
            jax.ShapeDtypeStruct((TOK, HEADS_DEV * HS), BF),
        ],
        in_specs=[hbm, hbm, hbm, hbm, hbm, vmem, smem],
        out_specs=[hbm, vmem],
        scratch_shapes=[
            pltpu.VMEM((1000, ZN, 16, HS), BF),
            pltpu.VMEM((DEV, 2, HS), I32),
            pltpu.VMEM((8, HS), I32),
            pltpu.SMEM((8, HS), I32),
            pltpu.VMEM((4, 4, 2, 4, 4, 64, HS), BF),
            pltpu.VMEM((4, 8, 4, 4, 64, HS), BF),
            pltpu.VMEM((4, 4, 8, 4, 64, HS), BF),
            pltpu.VMEM((4, 4, 4, 8, 64, HS), BF),
            pltpu.VMEM((4, IDS, DEV * CAP), BF),
            pltpu.VMEM((HEADS_DEV, DEV * CAP, 2 * HS), BF),
            pltpu.VMEM((SPAN, HS), BF),
            pltpu.VMEM((HALO + SPAN, HS), BF),
            pltpu.VMEM((HALO + SPAN, HS), BF),
            pltpu.VMEM((SPAN, HS), BF),
            pltpu.VMEM((TOK + STRETCH, HEADS_DEV * HS), BF),
            pltpu.VMEM((4, HEADS_DEV, STRETCH, HS), BF),
            pltpu.VMEM((5, HEADS_DEV, STRETCH, HS), BF),
            dma, dma((23,)), dma((23,)), dma, dma, dma, dma, dma,
            dma((2,)), dma((2,)), dma, dma((2,)), dma((4, 3, 3)), dma((4, 3, 3)),
            dma, dma, dma, dma,
        ],
        compiler_params=pltpu.CompilerParams(
            collective_id=0, has_side_effects=True, vmem_limit_bytes=62 * 1024 * 1024
        ),
        name="retrieval",
    )(queries, keys, values, cca_queries, view, neighbour_ids, doc_lengths)


def solution(mesh):
    in_specs = (
        P("seq", "heads"),
        P("seq", "heads"),
        P("seq", "heads"),
        P("seq", "heads"),
        P(("seq", "heads"), None, None),
        P(("seq", "heads"), None, None),
        P(),
    )
    out_specs = (P("seq", "heads"), P("seq", "heads"))

    def run(*args):
        return tuple(
            jax.shard_map(body, mesh=mesh, in_specs=in_specs, out_specs=out_specs, check_vma=False)(*args)
        )

    return run
```

```python
import functools
import math

import jax
import jax.numpy as jnp
from jax import lax
from jax.experimental import pallas as pl
from jax.experimental.pallas import tpu as pltpu
from jax.sharding import PartitionSpec as P

MESH = pl.DeviceIdType.MESH
BF = jnp.bfloat16
F32 = jnp.float32
I32 = jnp.int32

HS = 128
STRETCH = 64
NLEN = 128
IDS = 256
CAP = 4
SEQ = 32
ZN = 4
DEV = SEQ * ZN
GROUP = 8
TOK = 256
HEADS_DEV = 8
SPAN = GROUP * TOK
HALO = 1792
WIN = HALO + TOK
NEG = -1e30
LOG2E = 1.4426950408889634
FACTOR = LOG2E / math.sqrt(HS)


def dot(a, b, contract=(1, 0)):
    return lax.dot_general(
        a, b, (((contract[0],), (contract[1],)), ((), ())), preferred_element_type=F32
    )


def iota(shape, dim):
    return lax.broadcasted_iota(I32, shape, dim)


def drain(ref, sem):
    pltpu.make_async_copy(ref, ref, sem).wait()


ROUTES = (("x", "y", "z"), ("y", "z", "x"), ("z", "x", "y"))
GROUPS = ((0, 2), (2, 1), (3, 1))


def route(a, n):
    return ROUTES[(a + n) % 3]


def kernel(
    q, k, v, cq, table, ids, lens, att, done,
    tab, ids_all, plan_v, plan_s, out1, in1, in2, rows, picks, zbuf, qh, kh, vh, oh, cqs, cqq, oc,
    tab_sem, id_send, id_recv, plan_sem, qkv_send, q_recv, k_recv, v_recv,
    halo_send, halo_recv, cq_send, cq_recv, row_send, row_recv,
    o_send, o_recv, oc_send, oc_recv, done_sem,
):
    s = lax.axis_index("seq")
    z = lax.axis_index("heads")
    me = s * ZN + z
    y, x, c = s // 8, lax.rem(s // 2, 4), lax.rem(s, 2)
    here = {"x": x, "y": y, "z": z}
    g = lax.rem(s, GROUP)
    row = y
    ahead = lax.rem(s + 1, SEQ)
    behind = lax.rem(s + SEQ - 1, SEQ)

    def device(x2=x, y2=y, z2=z, c2=c):
        return (y2 * 4 + x2) * 2 + c2, z2

    def along(axis, n, dc=0):
        to = lax.rem(here[axis] + n, 4)
        return to, device(**{axis + "2": to, "c2": lax.rem(c + dc, 2)})

    def across(dy, dx):
        return device(x2=lax.rem(x + dx, 4), y2=lax.rem(y + dy, 4))

    table_copy = pltpu.make_async_copy(table, tab, tab_sem)
    table_copy.start()

    barrier = pltpu.get_barrier_semaphore()
    partners = [along("x", 0, 1)[1]]
    for axis in ("x", "y", "z"):
        for n in range(1, 4):
            for dc in range(2):
                partners.append(along(axis, n, dc)[1])
    partners += [across(dy, dx) for dy in range(1, 4) for dx in range(1, 4)]
    partners += [(ahead, z), (behind, z)]
    for other in partners:
        pl.semaphore_signal(barrier, inc=1, device_id=other, device_id_type=MESH)
    pl.semaphore_wait(barrier, len(partners))

    ids_all[me] = ids[0]

    def share(block, to, n):
        copy = pltpu.make_async_remote_copy(
            block, block, id_send.at[n], id_recv.at[n], device_id=to, device_id_type=MESH
        )
        copy.start()
        return copy

    first = [
        share(ids_all.at[me], along("z", n % 4, n // 4)[1], n) for n in range(1, 8)
    ]
    for copy in first:
        copy.wait()
    block = ids_all.at[pl.ds((y * 4 + x) * 8, 8)]
    second = [share(block, across(n // 4, n % 4), 7 + n) for n in range(1, 16)]

    for n in range(1, GROUP):
        to = lax.rem(g + n, GROUP)
        for src, dst, at, sem in (
            (q, qh, 0, q_recv), (k, kh, HALO, k_recv), (v, vh, HALO, v_recv),
        ):
            pltpu.make_async_remote_copy(
                src.at[:, pl.ds(to * HS, HS)], dst.at[pl.ds(at + g * TOK, TOK)],
                qkv_send, sem, device_id=(row * GROUP + to, z), device_id_type=MESH,
            ).start()
    for src, dst, at, sem in (
        (q, qh, 0, q_recv), (k, kh, HALO, k_recv), (v, vh, HALO, v_recv),
    ):
        pltpu.make_async_copy(
            src.at[:, pl.ds(g * HS, HS)], dst.at[pl.ds(at + g * TOK, TOK)], sem
        ).start()
    cq_copy = pltpu.make_async_remote_copy(
        cq.at[pl.ds(0, STRETCH)], cqs.at[pl.ds(TOK, STRETCH)], cq_send, cq_recv.at[0],
        device_id=(behind, z), device_id_type=MESH,
    )
    cq_copy.start()
    cq_own = pltpu.make_async_copy(cq, cqs.at[pl.ds(0, TOK)], cq_recv.at[1])
    cq_own.start()

    for copy in second:
        copy.wait()

    base = me * 1000
    row0 = ids_all[:, 0, :] - base
    row1 = ids_all[:, 1, :] - base
    mine0 = (row0 >= 0) & (row0 < 1000)
    mine1 = (row1 >= 0) & (row1 < 1000)
    flag0 = jnp.where(mine0, 1.0, 0.0).astype(BF)
    flag1 = jnp.where(mine1, 1.0, 0.0).astype(BF)
    tri = jnp.where(iota((HS, HS), 0) < iota((HS, HS), 1), 1.0, 0.0).astype(BF)
    full = jnp.ones((HS, HS), BF)
    rank0 = dot(flag0, tri)
    rank1 = dot(flag1, tri) + dot(flag0, full)
    plan = jnp.zeros((8, HS), I32)
    ones8 = jnp.ones((8, HS), BF)
    for n in range(CAP):
        pick = jnp.where(mine0 & (rank0 == float(n)), row0, 0) + jnp.where(
            mine1 & (rank1 == float(n)), row1, 0
        )
        high = dot(ones8, (pick >> 5).astype(F32).astype(BF), (1, 1))
        low = dot(ones8, (pick & 31).astype(F32).astype(BF), (1, 1))
        value = (high * 32.0 + low).astype(I32)
        plan = jnp.where(iota((8, HS), 0) == n, value, plan)
    plan_v[...] = plan
    plan_copy = pltpu.make_async_copy(plan_v, plan_s, plan_sem)
    plan_copy.start()
    plan_copy.wait()
    table_copy.wait()

    def fetch(a):
        def column(t, carry):
            spot = {"y": t // 8, "x": lax.rem(t // 2, 4), "z": slice(None)}
            c2 = lax.rem(t, 2)
            for i, (low, count) in enumerate(GROUPS):
                order = route(a, i)
                at = (a, spot[order[0]], c2, spot[order[1]], spot[order[2]])
                for n in range(low, low + count):
                    found = tab[jnp.clip(plan_s[n, t * ZN + a], 0, 999)]
                    out1[at + (slice(n * 16, (n + 1) * 16), slice(None))] = found
            return carry

        lax.fori_loop(0, SEQ, column, 0)

    def part_of(i):
        low, count = GROUPS[i]
        return pl.ds(low * 16, count * 16)

    def travel(a, phase):
        everything = slice(None)
        for i in range(3):
            axis, part = route(a, i)[phase], part_of(i)
            send, recv = row_send.at[a, phase, i], row_recv.at[a, phase, i]
            if phase == 0:
                hops = [(n, dc) for n in range(4) for dc in range(2)]
            else:
                hops = [(n, 0) for n in range(4)]
            for n, dc in hops[1:] + hops[:1]:
                to, dev = along(axis, n, dc)
                if phase == 0:
                    src = out1.at[a, to, lax.rem(c + dc, 2), :, :, part]
                    dst = in1.at[a, here[axis] * 2 + c, :, :, part]
                elif phase == 1:
                    src = in1.at[a, :, to, :, part]
                    dst = in2.at[a, here[axis], :, :, part]
                else:
                    src = in2.at[a, :, :, to, part]
                    dst = rows.at[a, here[axis], :, :, part]
                if (n, dc) == (0, 0):
                    pltpu.make_async_copy(src, dst, recv).start()
                else:
                    pltpu.make_async_remote_copy(
                        src, dst, send, recv, device_id=dev, device_id_type=MESH
                    ).start()

    landed = (in1, in2, rows)

    def arrive(a, phase):
        for i in range(3):
            drain(landed[phase].at[a, :, :, :, part_of(i)], row_recv.at[a, phase, i])

    for a in (3, 0, 1):
        fetch(a)
        travel(a, 0)
    fetch(2)

    def owner_of(value):
        return jnp.floor((value.astype(F32) + 0.5) * 0.001).astype(I32)

    before = iota((HS, HS), 1) < iota((HS, HS), 0)
    slot_no = iota((HS, DEV * CAP), 1).astype(F32)
    for a in range(4):
        wanted = owner_of(ids_all[s * ZN + a])
        lane = [jnp.broadcast_to(wanted[n : n + 1, :], (HS, HS)) for n in range(2)]
        col = [jnp.transpose(w) for w in lane]
        rank0 = jnp.sum(jnp.where((col[0] == lane[0]) & before, 1.0, 0.0), axis=1, keepdims=True)
        rank1 = jnp.sum(
            jnp.where((col[1] == lane[1]) & before, 1.0, 0.0)
            + jnp.where(col[1] == lane[0], 1.0, 0.0),
            axis=1, keepdims=True,
        )
        for n, rank in ((0, rank0), (1, rank1)):
            owner = col[n][:, :1]
            part = {"z": owner & 3, "x": (owner >> 3) & 3, "y": owner >> 5}
            spots = []
            for i in range(3):
                order = route(a, i)
                spot = part[order[2]] * 32 + part[order[1]] * 8 + part[order[0]] * 2
                spots.append((spot + ((owner >> 2) & 1)).astype(F32))
            spot = jnp.where(rank < 2.0, spots[0], jnp.where(rank < 3.0, spots[1], spots[2]))
            slot = spot * CAP + rank
            picks[a, n * HS : (n + 1) * HS, :] = jnp.where(slot_no == slot, 1.0, 0.0).astype(BF)

    drain(qh, q_recv)
    drain(kh.at[pl.ds(HALO, SPAN)], k_recv)
    drain(vh.at[pl.ds(HALO, SPAN)], v_recv)
    halos = []
    for n, ref in ((0, kh), (1, vh)):
        copy = pltpu.make_async_remote_copy(
            ref.at[pl.ds(HALO + TOK, HALO)], ref.at[pl.ds(0, HALO)],
            halo_send.at[n], halo_recv.at[n], device_id=along("y", 1)[1], device_id_type=MESH,
        )
        copy.start()
        halos.append(copy)

    cq_copy.wait()
    cq_own.wait()
    up = jnp.where(iota((STRETCH, HS), 1) == iota((STRETCH, HS), 0) + 63, 1.0, 0.0).astype(BF)
    for a in range(4):
        moved = dot(up, cqs[a * STRETCH : a * STRETCH + 2 * STRETCH, :]).astype(BF)
        for h in range(HEADS_DEV):
            cqq[a, h] = moved[:, h * HS : (h + 1) * HS]

    def onward(a, phase):
        arrive(a, phase)
        travel(a, phase + 1)

    onward(3, 0)
    travel(2, 0)
    onward(0, 0)

    for copy in halos:
        copy.wait()

    def self_block(i):
        first_query = row * SPAN + i * TOK
        query_pos = iota((1, TOK), 1) + first_query
        begin = jnp.zeros((1, TOK), I32)
        end = 0
        for d in range(32):
            end = end + lens[d]
            begin = jnp.where(query_pos >= end, end, begin)
        at = pl.multiple_of(i * TOK, TOK)
        key_pos = iota((WIN, TOK), 0) + (first_query - HALO)
        scores = dot(kh[pl.ds(at, WIN), :], qh[pl.ds(at, TOK), :], (1, 1))
        scores = jnp.where((key_pos >= begin) & (key_pos <= query_pos), scores, NEG)
        top = jnp.max(scores, axis=0, keepdims=True)
        weights = jnp.exp2((scores - top) * FACTOR)
        total = jnp.sum(weights, axis=0, keepdims=True)
        mixed = dot(vh[pl.ds(at, WIN), :], weights.astype(BF), (0, 0)) / total
        oh[pl.ds(at, TOK), :] = mixed.T.astype(BF)

    def self_out(i):
        at = pl.multiple_of(i * TOK, TOK)
        place_out = att.at[:, pl.ds(pl.multiple_of(g * HS, HS), HS)]

        @pl.when(i != g)
        def _():
            pltpu.make_async_remote_copy(
                oh.at[pl.ds(at, TOK)], place_out, o_send, o_recv,
                device_id=(row * GROUP + i, z), device_id_type=MESH,
            ).start()

        @pl.when(i == g)
        def _():
            pltpu.make_async_copy(oh.at[pl.ds(at, TOK)], place_out, o_recv).start()

    def turn(i, carry):
        self_block(i)
        self_out(i)
        return carry

    lax.fori_loop(0, 2, turn, 0)
    onward(3, 1)
    lax.fori_loop(2, 4, turn, 0)
    onward(1, 0)
    lax.fori_loop(4, 6, turn, 0)
    onward(0, 1)
    lax.fori_loop(6, 8, turn, 0)

    swap = jnp.where(
        (iota((256, 256), 0) // 16 == iota((256, 256), 1) % 16)
        & (iota((256, 256), 0) % 16 == iota((256, 256), 1) // 16),
        1.0, 0.0,
    ).astype(BF)

    def stretch(a):
        def turn_rows(n, carry):
            for m in range(8):
                spot = n * 16 + 2 * m
                parts = [
                    rows[a, n * 2 + m // 4, m % 4, j * 4 : (j + 1) * 4].reshape(256, HS)
                    for j in range(2)
                ]
                turned = dot(swap, jnp.concatenate(parts, axis=1)).astype(BF)
                for j in range(2):
                    for h in range(HEADS_DEV):
                        for kv in range(2):
                            piece = turned[
                                (2 * h + kv) * 16 : (2 * h + kv + 1) * 16, j * HS : (j + 1) * HS
                            ]
                            zbuf[h, pl.ds((spot + j) * 16, 16), kv * HS : (kv + 1) * HS] = piece
            return carry

        lax.fori_loop(0, 2, turn_rows, 0)
        pick = picks[a]

        def weigh(scores):
            weights = jnp.exp2((scores - jnp.max(scores, axis=1, keepdims=True)) * FACTOR)
            return weights, jnp.sum(weights, axis=1, keepdims=True)

        both = [dot(pick, zbuf[h]).astype(BF) for h in range(HEADS_DEV)]
        keys = [pair[:, :HS] for pair in both]
        halves = [
            [(pair[m * NLEN : (m + 1) * NLEN, :HS], pair[m * NLEN : (m + 1) * NLEN, HS:]) for m in range(2)]
            for pair in both
        ]
        enc_scores = [[dot(key, key, (1, 1)) for key, _ in two] for two in halves]
        cca_scores = [dot(cqq[a, h], keys[h], (1, 1)) for h in range(HEADS_DEV)]
        enc = [[weigh(scores) for scores in two] for two in enc_scores]
        cross = [weigh(scores) for scores in cca_scores]
        for h in range(HEADS_DEV):
            encoded = []
            for (weights, total), (_, val) in zip(enc[h], halves[h]):
                mixed = dot(weights.astype(BF), val) / total
                encoded.append((val.astype(F32) + mixed).astype(BF))
            weights, total = cross[h]
            mixed = dot(weights.astype(BF), jnp.concatenate(encoded, axis=0)) / total
            oc[a + 1, h] = mixed.astype(BF)

    def keep(n):
        pltpu.make_async_copy(oc.at[n], done.at[n], done_sem).start()

    arrive(3, 2)
    onward(2, 0)
    stretch(3)
    keep(4)
    oc_copy = pltpu.make_async_remote_copy(
        oc.at[4], oc.at[0], oc_send, oc_recv, device_id=(ahead, z), device_id_type=MESH
    )
    oc_copy.start()
    onward(1, 1)
    arrive(0, 2)
    stretch(0)
    keep(1)
    onward(2, 1)
    arrive(1, 2)
    stretch(1)
    keep(2)
    arrive(2, 2)
    stretch(2)
    keep(3)
    oc_copy.wait()
    keep(0)
    drain(done, done_sem)

    drain(att, o_recv)
    for _ in range(GROUP - 1):
        drain(oh.at[pl.ds(0, TOK)], o_send)
    for _ in range(3):
        drain(qh.at[pl.ds(0, HALO)], qkv_send)
    for a in range(4):
        for i in range(3):
            part = part_of(i)
            drain(in1.at[a, pl.ds(0, 7), :, :, part], row_send.at[a, 0, i])
            drain(in2.at[a, pl.ds(0, 3), :, :, part], row_send.at[a, 1, i])
            drain(rows.at[a, pl.ds(0, 3), :, :, part], row_send.at[a, 2, i])


def finish(att_in, done, att, cca):
    att[...] = att_in[...]
    s = lax.axis_index("seq")
    down = jnp.where(iota((STRETCH, HS), 1) == iota((STRETCH, HS), 0) + 1, 1.0, 0.0).astype(BF)
    for b in range(4):
        for h in range(HEADS_DEV):
            upper = done[b, h]
            if b == 0:
                upper = jnp.where(s == 0, jnp.zeros_like(upper), upper)
            pair = jnp.concatenate([upper, done[b + 1, h]], axis=0)
            cca[b * STRETCH : (b + 1) * STRETCH, h * HS : (h + 1) * HS] = dot(down, pair).astype(BF)


def body(queries, keys, values, cca_queries, token_table, neighbour_ids, doc_lengths):
    view = token_table.reshape(1000, 2, 32, HS).transpose(0, 2, 1, 3).reshape(1000, ZN, 16, HS)
    vmem = pl.BlockSpec(memory_space=pltpu.VMEM)
    hbm = pl.BlockSpec(memory_space=pl.ANY)
    smem = pl.BlockSpec(memory_space=pltpu.SMEM)
    dma = pltpu.SemaphoreType.DMA
    att, done = pl.pallas_call(
        kernel,
        out_shape=[
            jax.ShapeDtypeStruct((TOK, HEADS_DEV * HS), BF),
            jax.ShapeDtypeStruct((5, HEADS_DEV, STRETCH, HS), BF),
        ],
        in_specs=[hbm, hbm, hbm, hbm, hbm, vmem, smem],
        out_specs=[hbm, hbm],
        scratch_shapes=[
            pltpu.VMEM((1000, ZN, 16, HS), BF),
            pltpu.VMEM((DEV, 2, HS), I32),
            pltpu.VMEM((8, HS), I32),
            pltpu.SMEM((8, HS), I32),
            pltpu.VMEM((4, 4, 2, 4, 4, 64, HS), BF),
            pltpu.VMEM((4, 8, 4, 4, 64, HS), BF),
            pltpu.VMEM((4, 4, 8, 4, 64, HS), BF),
            pltpu.VMEM((4, 4, 4, 8, 64, HS), BF),
            pltpu.VMEM((4, IDS, DEV * CAP), BF),
            pltpu.VMEM((HEADS_DEV, DEV * CAP, 2 * HS), BF),
            pltpu.VMEM((SPAN, HS), BF),
            pltpu.VMEM((HALO + SPAN, HS), BF),
            pltpu.VMEM((HALO + SPAN, HS), BF),
            pltpu.VMEM((SPAN, HS), BF),
            pltpu.VMEM((TOK + STRETCH, HEADS_DEV * HS), BF),
            pltpu.VMEM((4, HEADS_DEV, STRETCH, HS), BF),
            pltpu.VMEM((5, HEADS_DEV, STRETCH, HS), BF),
            dma, dma((23,)), dma((23,)), dma, dma, dma, dma, dma,
            dma((2,)), dma((2,)), dma, dma((2,)), dma((4, 3, 3)), dma((4, 3, 3)),
            dma, dma, dma, dma, dma,
        ],
        compiler_params=pltpu.CompilerParams(
            collective_id=0, has_side_effects=True, vmem_limit_bytes=62 * 1024 * 1024
        ),
        name="retrieval",
    )(queries, keys, values, cca_queries, view, neighbour_ids, doc_lengths)
    out = jax.ShapeDtypeStruct((TOK, HEADS_DEV * HS), BF)
    return pl.pallas_call(
        finish,
        out_shape=[out, out],
        in_specs=[vmem, vmem],
        out_specs=[vmem, vmem],
        name="finish",
    )(att, done)


def solution(mesh):
    in_specs = (
        P("seq", "heads"),
        P("seq", "heads"),
        P("seq", "heads"),
        P("seq", "heads"),
        P(("seq", "heads"), None, None),
        P(("seq", "heads"), None, None),
        P(),
    )
    out_specs = (P("seq", "heads"), P("seq", "heads"))

    def run(*args):
        return tuple(
            jax.shard_map(body, mesh=mesh, in_specs=in_specs, out_specs=out_specs, check_vma=False)(*args)
        )

    return run
```
